512 devices in a mesh: ev: 64 (over y, z_lo, core), tile: 8 (over x, z_hi).
Axes of the slice: x: 4, y: 4, z: 16 (z_hi: 2, z_lo: 8; z = z_hi * 8 + z_lo), core: 2. Of those that a mesh axis runs over, the one named last changes fastest.
Arguments:
- phase_times: float32 [8, 128, 256], P('tile', 'ev'), may hold values from -512 to 512
- kernel_ids: int32 [8, 128, 256], P('tile', 'ev'), may hold values from 0 to 63
- block_ids: int32 [8, 128, 256], P('tile', 'ev'), may hold values from 0 to 1023
- dest_tiles: int32 [8, 128, 256, 1], P('tile', 'ev'), may hold values from 0 to 7; in each aligned block of 512 rows (0 to 511, 512 to 1023, ..., all dimensions but the last counted through in order) at most 128 rows name the same one
- station_counts: int32 [8, 128], P('tile', 'ev'), may hold values from 1 to 256, 24576 in all within a row
- weight_table: int32 [64, 128], replicated, may hold values from 1 to 256
- source_row: float32 [128], P('ev'), may hold values from -1024 to -128
- source_col: float32 [128], P('ev'), may hold values from 0 to 2048
- valid_cells: float32 [128, 512, 2048], P('ev', None, 'tile'), may hold values from 0 to 1
Outputs:
- slowness: float32 [512, 2048], P('ev', 'tile')
The draws below stay inside these ranges and needn't reach their ends.
Inputs may be any that keep to these rules, and one draw needn't show every extreme that they name: `dest_tiles`: among the 512 slots of one list part held by one device (its events, its index of tile, in order), no map tile is named by more than 128 slots, and in every draw some tile is named by exactly 128 of one device's slots. `station_counts`: in each list the counts over all events sum to 24576, and some event has all 256 slots live.
All inputs are finite; a program needn't handle non-finite values. No bound on the sum of `station_counts` on one device may be relied on, other than what follows from the above.
Results may differ from the reference program's by a relative error of at most 0.0003.
Values sent between devices are 32-bit elements; how exact they have to be, the bound alone decides.
No kernel may reach another device: no remote copies, remote signals or barrier semaphores. Data moves between devices by JAX's collectives and lax.ppermute only.
A program may use at most 64 MiB of HBM per device.

```python
import math
import jax
import jax.numpy as jnp
import numpy as np
from jax import lax

NX = 512
CY = 256
EV_DEV = 2
SPD = 256
KERN = 64
SWEEPS = 4
NY = 2048
EVENTS = 128
BLOCKS = 1024
CAP = 128
N_TILE = 8


def touch_ends(values, own_key, least, high):
    place = [jax.random.randint(jax.random.fold_in(own_key, axis), (), 0, length) for axis, length in enumerate(values.shape)]
    widest = values.shape.index(max(values.shape))
    beside = place[:widest] + [(place[widest] + 1) % values.shape[widest]] + place[widest + 1:]
    return values.at[tuple(place)].set(least).at[tuple(beside)].set(high)


def block_levels(rng, dims, shards, smallest, high):
    level, own = 1.0, jax.random.fold_in(rng, 6)
    for dim, blocks in shards:
        steps = jnp.exp(jax.random.uniform(jax.random.fold_in(own, dim), (blocks,), jnp.float32, smallest / len(shards), high / len(shards)))
        level = level * jnp.repeat(steps, dims[dim] // blocks).reshape([-1 if axis == dim else 1 for axis in range(len(dims))])
    return level


def split_up(count, total, most, skew):
    portions = [(1 << 20) // math.isqrt(grade ** skew) + 1 for grade in range(2, count + 1)]
    surplus, counts = total - most - (count - 1), [1] * (count - 1)
    while surplus > 0:
        free = [i for i in range(count - 1) if counts[i] < most]
        whole, budget = sum([portions[i] for i in free]), surplus
        for i in free:
            extra = min(most - counts[i], max(1, budget * portions[i] // whole), surplus)
            counts[i] = counts[i] + extra
            surplus = surplus - extra
    return np.array([most] + counts)


def ragged(rng, amount, total, reach, slope):
    if amount == 2:
        one = jax.random.randint(rng, (), max(1, total - reach), min(reach, total - 1) + 1)
        return jnp.stack([one, total - one])
    lengths = jnp.asarray(split_up(amount, total, reach, slope), jnp.int32)
    twos = (amount - 1) // 2
    donor, taker = lengths[1:1 + 2 * twos:2], lengths[2:2 + 2 * twos:2]
    slack = jnp.minimum(donor - 1, reach - taker)
    moved = jax.random.randint(jax.random.fold_in(rng, 1), (twos,), 0, 1 << 20) % (slack + 1)
    lengths = lengths.at[1:1 + 2 * twos:2].set(donor - moved).at[2:2 + 2 * twos:2].set(taker + moved)
    return lengths[jax.random.permutation(jax.random.fold_in(rng, 2), amount)]


def routed_block(stream_key, own, number, rows, amount, top, limit, lean):
    ranking = jax.random.permutation(stream_key, amount)
    crowded, ordinary = portions_of(amount, rows * top, limit, lean, True), portions_of(amount, rows * top, limit, lean, False)
    places = jnp.arange(amount)

    def named(lengths, rotation):
        used = int((lengths > 0).sum())
        fixed = max(1, used // 4)
        shifted = fixed + (places - fixed + rotation * (used - fixed)) % max(1, amount - fixed)
        return jnp.zeros((amount,), jnp.int32).at[ranking[jnp.where(places < fixed, places, shifted)]].set(jnp.asarray(lengths, jnp.int32))

    lengths = jnp.where(number % 4 == 0, named(crowded, number // 4), named(ordinary, number - number // 4 - 1))
    mixed = jax.random.permutation(jax.random.fold_in(own, 3), amount)
    giver, taker = mixed[0:amount // 2 * 2:2], mixed[1:amount // 2 * 2:2]
    room = jnp.minimum(lengths[giver] - 1, limit - lengths[taker]) // 2
    room = jnp.where((giver == ranking[0]) | (taker == ranking[0]) | (lengths[taker] == 0), 0, jnp.maximum(room, 0))
    shifted = jax.random.randint(jax.random.fold_in(own, 4), (amount // 2,), 0, 1 << 20) % (room + 1)
    lengths = lengths.at[giver].add(-shifted).at[taker].add(shifted)
    members = jnp.searchsorted(jnp.cumsum(lengths), jnp.arange(rows * top), side="right").astype(jnp.int32)
    table = members.reshape(top, rows).T
    table = table[jax.random.permutation(jax.random.fold_in(own, 1), rows)]
    rotation = jax.random.randint(jax.random.fold_in(own, 2), (rows, 1), 0, top)
    return jnp.take_along_axis(table, (jnp.arange(top)[None, :] + rotation) % top, axis=1)


def portions_of(count, total, limit, slope, full):
    weights = [(1 << 20) // math.isqrt(grade ** slope) + 1 for grade in range(1, count + 1)]
    largest = limit if full else min(limit, max(-(-total // count), total * weights[0] // sum(weights)))
    least = 1 if total - largest >= count - 1 else 0
    holding, surplus = [largest] + [least] * (count - 1), total - largest - least * (count - 1)
    while surplus > 0:
        free = [i for i in range(1, count) if holding[i] < largest] or [i for i in range(1, count) if holding[i] < limit]
        whole, left = sum([weights[i] for i in free]), surplus
        for i in free:
            addition = min(limit - holding[i], max(1, left * weights[i] // whole), surplus)
            holding[i] = holding[i] + addition
            surplus = surplus - addition
    return np.array(holding)


def noise(key, dims, deviation, reach, pieces=(), kind=jnp.bfloat16):
    result = jax.random.normal(key, dims, jnp.float32) * deviation
    if len(pieces) > 0:
        result = block_levels(key, dims, pieces, -0.22, 0.18) * result
    return jnp.clip(result, min=-reach, max=reach).astype(kind)


def setup_inputs(seed: int = 0) -> dict:
    streams_of = jax.random.split(jax.random.key(seed), 10)
    phase_times = noise(streams_of[0], (N_TILE, EVENTS, SPD), 80.0, 512.0, ((0, 8), (1, 64)), jnp.float32)
    kernel_ids = touch_ends(jax.random.randint(streams_of[1], (N_TILE, EVENTS, SPD), 0, KERN), jax.random.fold_in(streams_of[1], 1), 0, KERN - 1).astype(jnp.int32)
    block_ids = touch_ends(jax.random.randint(streams_of[2], (N_TILE, EVENTS, SPD), 0, BLOCKS), jax.random.fold_in(streams_of[2], 1), 0, BLOCKS - 1).astype(jnp.int32)
    dest_tiles_keys = jax.random.split(jax.random.fold_in(streams_of[3], 1), N_TILE * EVENTS * SPD // (EV_DEV * SPD))
    dest_tiles_turns = jax.random.permutation(jax.random.fold_in(streams_of[3], 3), N_TILE * EVENTS * SPD // (EV_DEV * SPD))
    dest_tiles = jax.vmap(lambda own, number: routed_block(jax.random.fold_in(streams_of[3], 2), own, number, EV_DEV * SPD, N_TILE, 1, CAP, 1))(dest_tiles_keys, dest_tiles_turns).reshape((N_TILE, EVENTS, SPD, 1))
    station_counts = jax.vmap(lambda own: ragged(own, EVENTS, 3 * EVENTS * SPD // 4, SPD, 2))(jax.random.split(streams_of[4], N_TILE)).reshape((N_TILE, EVENTS)).astype(jnp.int32)
    weight_table = touch_ends(jax.random.randint(streams_of[5], (KERN, 128), 1, 257), jax.random.fold_in(streams_of[5], 1), 1, 256).astype(jnp.int32)
    source_row = jnp.clip(-1024.0 + 896.0 * jax.random.uniform(streams_of[6], (EVENTS,), jnp.float32) ** block_levels(streams_of[6], (EVENTS,), ((0, 64),), -0.2, 0.2), -1024.0, -128.0)
    source_col = jnp.clip(2048.0 * jax.random.uniform(streams_of[7], (EVENTS,), jnp.float32) ** block_levels(streams_of[7], (EVENTS,), ((0, 64),), -0.2, 0.2), 0.0, 2048.0)
    valid_cells = jnp.clip(1.0 * jax.random.uniform(streams_of[8], (EVENTS, NX, NY), jnp.float32) ** block_levels(streams_of[8], (EVENTS, NX, NY), ((0, 64), (2, 8)), -0.2, 0.2), 0.0, 1.0)
    return dict(phase_times=phase_times, kernel_ids=kernel_ids, block_ids=block_ids, dest_tiles=dest_tiles, station_counts=station_counts, weight_table=weight_table, source_row=source_row, source_col=source_col, valid_cells=valid_cells)


SMOOTH = 0.024

def laplace(values):
    padded = jnp.pad(values, ((0, 0), (1, 1), (1, 1)))
    beside_all = padded[:, :-2, 1:-1] + padded[:, 2:, 1:-1] + padded[:, 1:-1, :-2] + padded[:, 1:-1, 2:]
    return beside_all - 4.0 * values

def speed_field(margin, row_pos, col_pos, src_rows, src_cols):
    rows_padded = jnp.pad(margin, ((0, 0), (1, 1), (0, 0)))
    grad_row = 0.5 * (rows_padded[:, 2:, 1:-1] - rows_padded[:, :-2, 1:-1])
    grad_col = 0.5 * (margin[:, :, 2:] - margin[:, :, :-2])
    off_row = row_pos[None, :, None] - src_rows[:, None, None]
    off_col = col_pos[None, None, :] - src_cols[:, None, None]
    distance = jnp.sqrt(off_row * off_row + off_col * off_col)
    along_row = off_row / distance + grad_row
    along_col = off_col / distance + grad_col
    return jnp.sqrt(along_row * along_row + along_col * along_col)

def reference(phase_times, kernel_ids, block_ids, dest_tiles, station_counts, weight_table, source_row, source_col, valid_cells):
    segments = CY // 128
    lane_index = jnp.arange(128, dtype=jnp.int32)
    slot_index = jnp.arange(SPD, dtype=jnp.int32)
    row_pos = jnp.arange(NX, dtype=jnp.float32)
    col_pos = jnp.arange(NY, dtype=jnp.float32)
    kernel_table = weight_table.astype(jnp.float32) * (1.0 / 256.0)

    def one_event(totals, inputs):
        stacked, hit_count = totals
        event_times, event_kernel, event_block, event_dest, event_count, event_row, event_col, event_valid = inputs
        live_slot = (slot_index[None, :] < event_count[:, None]).astype(jnp.float32)
        weights = kernel_table[event_kernel] * live_slot[:, :, None]
        grid_row = event_block // segments
        grid_col = event_dest * CY + event_block % segments * 128
        flat_index = ((grid_row * NY + grid_col)[:, :, None] + lane_index[None, None, :]).reshape(-1)
        numerator = jnp.zeros((NX * NY,), jnp.float32).at[flat_index].add((weights * event_times[:, :, None]).reshape(-1))
        weight_sum = jnp.zeros((NX * NY,), jnp.float32).at[flat_index].add(weights.reshape(-1))
        numerator = numerator.reshape(1, NX, NY)
        weight_sum = weight_sum.reshape(1, NX, NY)
        change = SMOOTH * numerator
        for sweep_index in range(SWEEPS - 1):
            curvature = laplace(change)
            bending = laplace(curvature)
            change = change - SMOOTH * (bending + weight_sum * change - numerator)
        margin = jnp.pad(change, ((0, 0), (0, 0), (1, 1)))
        wave_speed = speed_field(margin, row_pos, col_pos, event_row[None], event_col[None])[0]
        return ((stacked + event_valid * wave_speed, hit_count + event_valid), None)
    inputs = (jnp.transpose(phase_times, (1, 0, 2)), jnp.transpose(kernel_ids, (1, 0, 2)), jnp.transpose(block_ids, (1, 0, 2)), jnp.transpose(dest_tiles[:, :, :, 0], (1, 0, 2)), jnp.transpose(station_counts, (1, 0)), source_row, source_col, valid_cells)
    start = (jnp.zeros((NX, NY), jnp.float32), jnp.zeros((NX, NY), jnp.float32))
    (stacked, hit_count), unused = lax.scan(one_event, start, inputs)
    return stacked / (1.0 + hit_count)
```

```python
import functools

import jax
import jax.numpy as jnp
import numpy as np
from jax import lax
from jax.experimental import pallas as pl
from jax.experimental.pallas import tpu as pltpu
from jax.sharding import Mesh
from jax.sharding import PartitionSpec as P

SWEEPS = 4
SMOOTH = 0.024

YS, ZS, CS, XS, WS = 4, 8, 2, 4, 2
EV, TILE = ("y", "z", "c"), ("x", "w")
LISTS = XS * WS

EVENTS, SLOTS, ROWS, COLS, LANES = 2, 256, 512, 256, 128
KERN = 64
SHARE = ROWS // (YS * ZS * CS)
PAD = 8
TILES = 3
CHUNK = 64


def pack(times, kernels, blocks, dests, counts, out):
    lane = lax.broadcasted_iota(jnp.int32, (1, LANES), 1)
    for e in range(EVENTS):
        for h in range(2):
            part = slice(h * LANES, (h + 1) * LANES)
            live = lane + h * LANES < counts[0, e]
            k = 2 * e + h
            out[0, k : k + 1, :] = times[0, e : e + 1, part]
            out[0, 4 + k : 5 + k, :] = jnp.where(live, kernels[0, e : e + 1, part], -1).astype(jnp.float32)
            out[0, 8 + k : 9 + k, :] = blocks[0, e : e + 1, part].astype(jnp.float32)
            out[0, 12 + k : 13 + k, :] = dests[e : e + 1, part].astype(jnp.float32)
    for p in range(1, LISTS):
        out[p] = out[0]


def gather_maps(arrived, table, tile, onehot, cells, weights, numer):
    f32, bf16 = jnp.float32, jnp.bfloat16
    table_t = jnp.transpose(table[...].astype(f32)).astype(bf16)
    pick = lax.broadcasted_iota(jnp.int32, (KERN, SLOTS), 0)
    row_of = lax.broadcasted_iota(jnp.int32, (ROWS, SLOTS), 0)
    lane = lax.broadcasted_iota(jnp.int32, (1, LANES), 1)

    for e in range(EVENTS):

        def one_list(t, carry, e=e):
            def both(k):
                k = k + 2 * e
                return jnp.concatenate([arrived[t, k : k + 1, :], arrived[t, k + 1 : k + 2, :]], axis=1)

            time = both(0)
            kernel = both(4).astype(jnp.int32)
            block = both(8).astype(jnp.int32)
            dest = both(12).astype(jnp.int32)
            seg = dest * 2 + (block & 1) - 2 * tile
            row = block >> 1
            at = pl.ds(pl.multiple_of(t * SLOTS, SLOTS), SLOTS)
            onehot[:, at] = jnp.where(row_of == row, 1.0, 0.0).astype(bf16)
            picked = jnp.where(pick == kernel, 1.0, 0.0).astype(bf16)
            w = jnp.dot(table_t, picked, preferred_element_type=f32) * (1.0 / 256.0)
            v = w * time
            v_hi = v.astype(bf16).astype(f32)
            v_lo = v - v_hi
            for k, part in enumerate((w, v_hi, v_lo)):
                for h in range(2):
                    cells[pl.ds((2 * k + h) * LANES, LANES), at] = jnp.where(seg == h, part, 0.0).astype(bf16)
            right, left = seg == 2, seg == -1
            border = [jnp.where(right, part[:8], 0.0) for part in (w, v_hi, v_lo)]
            border.append(jnp.zeros((80, SLOTS), f32))
            border += [jnp.where(left, part[LANES - 8 :], 0.0) for part in (v_lo, v_hi, w)]
            cells[pl.ds(6 * LANES, LANES), at] = jnp.concatenate(border, axis=0).astype(bf16)
            return carry

        lax.fori_loop(0, LISTS, one_list, 0)

        for r in range(0, ROWS, 256):
            sums = lax.dot_general(
                onehot[r : r + 256, :], cells[...], (((1,), (1,)), ((), ())), preferred_element_type=f32
            )
            for h in range(2):
                cut = lambda k: sums[:, (2 * k + h) * LANES : (2 * k + h + 1) * LANES]
                weights[TILES * e + h, r : r + 256, :] = cut(0)
                numer[TILES * e + h, r : r + 256, :] = cut(1) + cut(2)
            edge = sums[:, 6 * LANES :]
            beside = (lane < 8) | (lane >= LANES - 8)
            right = pltpu.roll(edge, LANES - 8, 1) + pltpu.roll(edge, LANES - 16, 1)
            left = pltpu.roll(edge, 8, 1) + pltpu.roll(edge, 16, 1)
            weights[TILES * e + 2, r : r + 256, :] = jnp.where(beside, edge, 0.0)
            numer[TILES * e + 2, r : r + 256, :] = jnp.where(
                lane < 8, right, jnp.where(lane >= LANES - 8, left, 0.0)
            )


def beside(tiles, lane):
    up = [pltpu.roll(x, 1, 1) for x in tiles]
    down = [pltpu.roll(x, LANES - 1, 1) for x in tiles]
    n = len(tiles)
    left = [jnp.where(lane == 0, up[(j + n - 1) % n], up[j]) for j in range(n)]
    right = [jnp.where(lane == LANES - 1, down[(j + 1) % n], down[j]) for j in range(n)]
    return left, right


def laplace_of(buf, first, r0, lane):
    near = [buf[first + j, pl.ds(r0 + PAD, CHUNK), :] for j in range(TILES)]
    left, right = beside(near, lane)
    out = []
    for j in range(TILES):
        above = buf[first + j, pl.ds(r0 + PAD - 1, CHUNK), :]
        below = buf[first + j, pl.ds(r0 + PAD + 1, CHUNK), :]
        out.append((above + below) + (left[j] + right[j]) - 4.0 * near[j])
    return out


def work(
    arrived, table, source_row, source_col, valid_hbm, send, keep,
    onehot, cells, weights, numer, change, curve, valid, arrival,
):
    tile = lax.axis_index("x") * WS + lax.axis_index("w")
    core = lax.axis_index("c")
    copy = pltpu.make_async_copy(valid_hbm, valid, arrival)
    copy.start()
    gather_maps(arrived, table, tile, onehot, cells, weights, numer)

    lane = lax.broadcasted_iota(jnp.int32, (1, LANES), 1)
    half = LANES // 2
    inside = jnp.where(((tile == 0) & (lane >= half)) | ((tile == LISTS - 1) & (lane < half)), 0.0, 1.0)
    empty = jnp.zeros((PAD, LANES), jnp.float32)
    for k in range(EVENTS * TILES):
        for buf in (change, curve):
            buf[k, 0:PAD, :] = empty
            buf[k, ROWS + PAD : ROWS + 2 * PAD, :] = empty
    spans = ROWS // CHUNK

    def first_sweep(i, carry):
        r0 = pl.multiple_of(i * CHUNK, CHUNK)
        for k in range(EVENTS * TILES):
            change[k, pl.ds(r0 + PAD, CHUNK), :] = SMOOTH * numer[k, pl.ds(r0, CHUNK), :]
        return carry

    lax.fori_loop(0, spans, first_sweep, 0)

    def curve_pass(i, carry):
        r0 = pl.multiple_of(i * CHUNK, CHUNK)
        for e in range(EVENTS):
            laps = laplace_of(change, TILES * e, r0, lane)
            laps[2] = laps[2] * inside
            for j in range(TILES):
                curve[TILES * e + j, pl.ds(r0 + PAD, CHUNK), :] = laps[j]
        return carry

    def update_pass(i, carry):
        r0 = pl.multiple_of(i * CHUNK, CHUNK)
        for e in range(EVENTS):
            bends = laplace_of(curve, TILES * e, r0, lane)
            for j in range(TILES):
                k = TILES * e + j
                at = pl.ds(r0 + PAD, CHUNK)
                old = change[k, at, :]
                pull = weights[k, pl.ds(r0, CHUNK), :] * old - numer[k, pl.ds(r0, CHUNK), :]
                new = old - SMOOTH * (bends[j] + pull)
                change[k, at, :] = new * inside if j == 2 else new
        return carry

    def sweep(s, carry):
        lax.fori_loop(0, spans, curve_pass, 0)
        lax.fori_loop(0, spans, update_pass, 0)
        return carry

    lax.fori_loop(0, SWEEPS - 1, sweep, 0)
    copy.wait()

    column = lax.broadcasted_iota(jnp.int32, (1, LANES), 1) + tile * COLS
    line = lax.broadcasted_iota(jnp.int32, (SHARE, 1), 0)

    def stack(out, core_of):
        def one_share(g, carry):
            r0 = pl.multiple_of(g * (CS * SHARE) + core_of * SHARE, SHARE)
            total = [jnp.zeros((SHARE, LANES), jnp.float32) for h in range(2)]
            hits = [jnp.zeros((SHARE, LANES), jnp.float32) for h in range(2)]
            for e in range(EVENTS):
                near = [change[TILES * e + j, pl.ds(r0 + PAD, SHARE), :] for j in range(TILES)]
                left, right = beside(near, lane)
                off_row = (line + r0).astype(jnp.float32) - source_row[e]
                for h in range(2):
                    above = change[TILES * e + h, pl.ds(r0 + PAD - 1, SHARE), :]
                    below = change[TILES * e + h, pl.ds(r0 + PAD + 1, SHARE), :]
                    off_col = (column + h * LANES).astype(jnp.float32) - source_col[e]
                    inverse = lax.rsqrt(off_row * off_row + off_col * off_col)
                    along_row = off_row * inverse + 0.5 * (below - above)
                    along_col = off_col * inverse + 0.5 * (right[h] - left[h])
                    speed = jnp.sqrt(along_row * along_row + along_col * along_col)
                    cell = valid[e, pl.ds(r0, SHARE), h * LANES : (h + 1) * LANES]
                    total[h] = total[h] + cell * speed
                    hits[h] = hits[h] + cell
            for h in range(2):
                part = slice(h * LANES, (h + 1) * LANES)
                out[g, 0, :, part] = total[h]
                out[g, 1, :, part] = hits[h]
            return carry

        lax.fori_loop(0, YS * ZS, one_share, 0)

    stack(send, 1 - core)
    stack(keep, core)


def maps_of(arrived, table, source_row, source_col, valid):
    f32 = jnp.float32
    shares = jax.ShapeDtypeStruct((YS * ZS, 2, SHARE, COLS), f32)
    vmem, smem = pl.BlockSpec(memory_space=pltpu.VMEM), pl.BlockSpec(memory_space=pltpu.SMEM)
    wide = pltpu.VMEM((EVENTS * TILES, ROWS, LANES), f32)
    padded = pltpu.VMEM((EVENTS * TILES, ROWS + 2 * PAD, LANES), f32)
    return pl.pallas_call(
        work,
        out_shape=(shares, shares),
        in_specs=[vmem, vmem, smem, smem, pl.BlockSpec(memory_space=pl.ANY)],
        out_specs=(vmem, vmem),
        scratch_shapes=[
            pltpu.VMEM((ROWS, LISTS * SLOTS), jnp.bfloat16),
            pltpu.VMEM((7 * LANES, LISTS * SLOTS), jnp.bfloat16),
            wide, wide, padded, padded,
            pltpu.VMEM((EVENTS, ROWS, COLS), f32),
            pltpu.SemaphoreType.DMA,
        ],
        compiler_params=pltpu.CompilerParams(vmem_limit_bytes=40 * 1024 * 1024),
        name="maps",
    )(arrived, table, source_row, source_col, valid)


def packed(times, kernels, blocks, dests, counts):
    vmem, smem = pl.BlockSpec(memory_space=pltpu.VMEM), pl.BlockSpec(memory_space=pltpu.SMEM)
    return pl.pallas_call(
        pack,
        out_shape=jax.ShapeDtypeStruct((LISTS, 16, LANES), jnp.float32),
        in_specs=[vmem, vmem, vmem, vmem, smem],
        out_specs=vmem,
        name="pack",
    )(times, kernels, blocks, dests, counts)


def on_device(times, kernels, blocks, dests, counts, table, source_row, source_col, valid):
    outgoing = packed(times, kernels, blocks, dests.reshape(EVENTS, SLOTS), counts)
    arrived = lax.all_to_all(outgoing, TILE, 0, 0, tiled=True)
    send, keep = maps_of(arrived, table, source_row, source_col, valid)
    both = keep + lax.ppermute(send, "c", [(0, 1), (1, 0)])
    both = both.reshape(YS, ZS, 2, SHARE, COLS)
    both = jnp.sum(lax.all_to_all(both, "y", 0, 0, tiled=True), axis=0)
    both = jnp.sum(lax.all_to_all(both, "z", 0, 0, tiled=True), axis=0)
    return both[0] / (1.0 + both[1])


def solution(mesh):
    split = Mesh(np.asarray(mesh.devices).reshape(YS, ZS, CS, XS, WS), EV + TILE)
    placed = (
        P(TILE, EV, None),
        P(TILE, EV, None),
        P(TILE, EV, None),
        P(TILE, EV, None, None),
        P(TILE, EV),
        P(),
        P(EV),
        P(EV),
        P(EV, None, TILE),
    )
    return jax.shard_map(on_device, mesh=split, in_specs=placed, out_specs=P(EV, TILE), check_vma=False)
```

```python
import functools

import jax
import jax.numpy as jnp
import numpy as np
from jax import lax
from jax.experimental import pallas as pl
from jax.experimental.pallas import tpu as pltpu
from jax.sharding import Mesh
from jax.sharding import PartitionSpec as P

SWEEPS = 4
SMOOTH = 0.024

YS, ZS, CS, XS, WS = 4, 8, 2, 4, 2
EV, TILE = ("y", "z", "c"), ("x", "w")
LISTS = XS * WS
UNROLL = 8

EVENTS, SLOTS, ROWS, COLS, LANES = 2, 256, 512, 256, 128
KERN = 64
SHARE = ROWS // (YS * ZS * CS)
PAD = 8
EDGE = 8
SPAN = COLS + 2 * EDGE
LINES = ROWS // LANES
BLOCK = 32


def pack(times, kernels, blocks, dests, counts, out):
    lane = lax.broadcasted_iota(jnp.int32, (1, LANES), 1)
    for e in range(EVENTS):
        for h in range(2):
            part = slice(h * LANES, (h + 1) * LANES)
            live = lane + h * LANES < counts[0, e]
            k = 2 * e + h
            out[0, k : k + 1, :] = times[0, e : e + 1, part]
            out[0, 4 + k : 5 + k, :] = jnp.where(live, kernels[0, e : e + 1, part], -1).astype(jnp.float32)
            out[0, 8 + k : 9 + k, :] = blocks[0, e : e + 1, part].astype(jnp.float32)
            out[0, 12 + k : 13 + k, :] = dests[e, :, part].astype(jnp.float32)
    for p in range(1, LISTS):
        out[p] = out[0]


def gather_maps(arrived, table, tile, onehot, cells, weights, numer, change):
    f32, bf16 = jnp.float32, jnp.bfloat16
    columns = jnp.transpose(table[...].astype(f32)) * (1.0 / 256.0)
    none = jnp.zeros((LANES, KERN), f32)
    by_segment = jnp.concatenate(
        [
            jnp.concatenate([columns[LANES - EDGE :]] + [none[:EDGE]] * 3, axis=1),
            jnp.concatenate([none, columns, none, none], axis=1),
            jnp.concatenate([none, none, columns, none], axis=1),
            jnp.concatenate([none[:EDGE]] * 3 + [columns[:EDGE]], axis=1),
        ],
        axis=0,
    ).astype(bf16)
    pick = lax.broadcasted_iota(jnp.int32, (4 * KERN, SLOTS), 0)
    row_of = lax.broadcasted_iota(jnp.int32, (ROWS, SLOTS), 0)

    for e in range(EVENTS):

        def one_list(t, carry, e=e):
            def both(k):
                k = k + 2 * e
                return jnp.concatenate([arrived[t, k : k + 1, :], arrived[t, k + 1 : k + 2, :]], axis=1)

            time = both(0)
            kernel = both(4).astype(jnp.int32)
            block = both(8).astype(jnp.int32)
            dest = both(12).astype(jnp.int32)
            seg = dest * 2 + (block & 1) - 2 * tile + 1
            row = block >> 1
            place = (row & (LINES - 1)) * LANES + row // LINES
            choice = jnp.where((kernel >= 0) & (seg >= 0) & (seg < 4), seg * KERN + kernel, -1)
            at = pl.ds(pl.multiple_of(t * SLOTS, SLOTS), SLOTS)
            onehot[:, at] = jnp.where(row_of == place, 1.0, 0.0).astype(bf16)
            picked = jnp.where(pick == choice, 1.0, 0.0).astype(bf16)
            w = jnp.dot(by_segment, picked, preferred_element_type=f32)
            v = w * time
            v_hi = v.astype(bf16)
            cells[0:SPAN, at] = w.astype(bf16)
            cells[SPAN : 2 * SPAN, at] = v_hi
            cells[2 * SPAN : 3 * SPAN, at] = (v - v_hi.astype(f32)).astype(bf16)
            return carry

        lax.fori_loop(0, LISTS, one_list, 0, unroll=UNROLL)

        def total(k):
            return lax.dot_general(
                cells[k * SPAN : (k + 1) * SPAN, :], onehot[...], (((1,), (1,)), ((), ())), preferred_element_type=f32
            )

        weight = total(0)
        number = total(1) + total(2)
        for t in range(LINES):
            part = slice(t * LANES, (t + 1) * LANES)
            weights[e, t] = weight[:, part]
            numer[e, t] = number[:, part]
            change[e, t, PAD : PAD + SPAN, :] = SMOOTH * number[:, part]


def beside(tiles, lane):
    first = jnp.where(lane == 0, 0.0, pltpu.roll(tiles[-1], 1, 1))
    last = jnp.where(lane == LANES - 1, 0.0, pltpu.roll(tiles[0], LANES - 1, 1))
    return [first] + tiles[:-1], tiles[1:] + [last]


def laplace_of(buf, e, p, size, lane):
    near = [buf[e, t, PAD + p : PAD + p + size, :] for t in range(LINES)]
    above, below = beside(near, lane)
    out = []
    for t in range(LINES):
        left = buf[e, t, PAD + p - 1 : PAD + p - 1 + size, :]
        right = buf[e, t, PAD + p + 1 : PAD + p + 1 + size, :]
        out.append((left + right) + (above[t] + below[t]) - 4.0 * near[t])
    return out


def work(
    arrived, table, source_row, source_col, valid_hbm, send, keep,
    onehot, cells, weights, numer, change, curve, valid, stacked, arrivals,
):
    f32 = jnp.float32
    tile = lax.axis_index("x") * WS + lax.axis_index("w")
    core = lax.axis_index("c")
    copies = [
        pltpu.make_async_copy(
            valid_hbm.at[e, :, h * LANES : (h + 1) * LANES], valid.at[e, h], arrivals.at[2 * e + h]
        )
        for e in range(EVENTS)
        for h in range(2)
    ]
    for copy in copies:
        copy.start()
    empty = jnp.zeros((PAD, LANES), f32)
    for buf in (change, curve):
        for e in range(EVENTS):
            for t in range(LINES):
                buf[e, t, 0:PAD, :] = empty
                buf[e, t, PAD + SPAN :, :] = empty
    gather_maps(arrived, table, tile, onehot, cells, weights, numer, change)

    lane = lax.broadcasted_iota(jnp.int32, (1, LANES), 1)
    parts = [(p, min(BLOCK, SPAN - p)) for p in range(0, SPAN, BLOCK)]

    def outside(buf, e):
        @pl.when(tile == 0)
        def _():
            for t in range(LINES):
                buf[e, t, PAD : PAD + EDGE, :] = empty

        @pl.when(tile == LISTS - 1)
        def _():
            for t in range(LINES):
                buf[e, t, PAD + SPAN - EDGE : PAD + SPAN, :] = empty

    def curve_pass(e, carry):
        for p, size in parts:
            for t, lap in enumerate(laplace_of(change, e, p, size, lane)):
                curve[e, t, PAD + p : PAD + p + size, :] = lap
        outside(curve, e)
        return carry

    def update_pass(e, carry):
        for p, size in parts:
            for t, bend in enumerate(laplace_of(curve, e, p, size, lane)):
                old = change[e, t, PAD + p : PAD + p + size, :]
                pull = weights[e, t, p : p + size, :] * old - numer[e, t, p : p + size, :]
                change[e, t, PAD + p : PAD + p + size, :] = old - SMOOTH * (bend + pull)
        outside(change, e)
        return carry

    def sweep(s, carry):
        lax.fori_loop(0, EVENTS, curve_pass, 0)
        lax.fori_loop(0, EVENTS, update_pass, 0)
        return carry

    lax.fori_loop(0, SWEEPS - 1, sweep, 0)
    for copy in copies:
        copy.wait()

    lines = lax.broadcasted_iota(jnp.int32, (1, LANES), 1) * LINES
    column = lax.broadcasted_iota(jnp.int32, (LANES, 1), 0) + tile * COLS

    def stack(h, carry):
        p = pl.multiple_of(PAD + EDGE + h * LANES, 8)
        totals = [None] * LINES
        for e in range(EVENTS):
            near = [change[e, t, pl.ds(p, LANES), :] for t in range(LINES)]
            above, below = beside(near, lane)
            off_col = (column + h * LANES).astype(f32) - source_col[e]
            for t in range(LINES):
                left = change[e, t, pl.ds(p - 1, LANES), :]
                right = change[e, t, pl.ds(p + 1, LANES), :]
                off_row = (lines + t).astype(f32) - source_row[e]
                inverse = lax.rsqrt(off_row * off_row + off_col * off_col)
                along_row = off_row * inverse + 0.5 * (below[t] - above[t])
                along_col = off_col * inverse + 0.5 * (right - left)
                speed = jnp.sqrt(along_row * along_row + along_col * along_col)
                term = valid[e, h, pl.ds(t, LANES, stride=LINES), :] * jnp.transpose(speed)
                totals[t] = term if e == 0 else totals[t] + term
        for t in range(LINES):
            stacked[h, pl.ds(t, LANES, stride=LINES), :] = totals[t]
        return carry

    lax.fori_loop(0, 2, stack, 0)

    def deal(out, core_of):
        def one_share(g, carry):
            at = pl.ds(pl.multiple_of(g * (CS * SHARE) + core_of * SHARE, SHARE), SHARE)
            for h in range(2):
                part = slice(h * LANES, (h + 1) * LANES)
                out[g, 0, :, part] = stacked[h, at, :]
                out[g, 1, :, part] = valid[0, h, at, :] + valid[1, h, at, :]
            return carry

        lax.fori_loop(0, YS * ZS, one_share, 0, unroll=8)

    deal(send, 1 - core)
    deal(keep, core)


def maps_of(arrived, table, source_row, source_col, valid):
    f32 = jnp.float32
    shares = jax.ShapeDtypeStruct((YS * ZS, 2, SHARE, COLS), f32)
    vmem, smem = pl.BlockSpec(memory_space=pltpu.VMEM), pl.BlockSpec(memory_space=pltpu.SMEM)
    wide = pltpu.VMEM((EVENTS, LINES, SPAN, LANES), f32)
    padded = pltpu.VMEM((EVENTS, LINES, SPAN + 2 * PAD, LANES), f32)
    return pl.pallas_call(
        work,
        out_shape=(shares, shares),
        in_specs=[vmem, vmem, smem, smem, pl.BlockSpec(memory_space=pltpu.HBM)],
        out_specs=(vmem, vmem),
        scratch_shapes=[
            pltpu.VMEM((ROWS, LISTS * SLOTS), jnp.bfloat16),
            pltpu.VMEM((3 * SPAN, LISTS * SLOTS), jnp.bfloat16),
            wide, wide, padded, padded,
            pltpu.VMEM((EVENTS, 2, ROWS, LANES), f32),
            pltpu.VMEM((2, ROWS, LANES), f32),
            pltpu.SemaphoreType.DMA((2 * EVENTS,)),
        ],
        compiler_params=pltpu.CompilerParams(vmem_limit_bytes=40 * 1024 * 1024),
        name="maps",
    )(arrived, table, source_row, source_col, valid)


def packed(times, kernels, blocks, dests, counts):
    vmem, smem = pl.BlockSpec(memory_space=pltpu.VMEM), pl.BlockSpec(memory_space=pltpu.SMEM)
    return pl.pallas_call(
        pack,
        out_shape=jax.ShapeDtypeStruct((LISTS, 16, LANES), jnp.float32),
        in_specs=[vmem, vmem, vmem, vmem, smem],
        out_specs=vmem,
        name="pack",
    )(times, kernels, blocks, dests, counts)


def on_device(times, kernels, blocks, dests, counts, table, source_row, source_col, valid):
    outgoing = packed(times, kernels, blocks, dests.reshape(EVENTS, 1, SLOTS), counts)
    arrived = lax.all_to_all(outgoing, TILE, 0, 0, tiled=True)
    send, keep = maps_of(arrived, table, source_row, source_col, valid)
    both = keep + lax.ppermute(send, "c", [(0, 1), (1, 0)])
    both = both.reshape(YS, ZS, 2, SHARE, COLS)
    both = jnp.sum(lax.all_to_all(both, "y", 0, 0, tiled=True), axis=0)
    both = jnp.sum(lax.all_to_all(both, "z", 0, 0, tiled=True), axis=0)
    return both[0] / (1.0 + both[1])


def solution(mesh):
    split = Mesh(np.asarray(mesh.devices).reshape(YS, ZS, CS, XS, WS), EV + TILE)
    placed = (
        P(TILE, EV, None),
        P(TILE, EV, None),
        P(TILE, EV, None),
        P(TILE, EV, None, None),
        P(TILE, EV),
        P(),
        P(EV),
        P(EV),
        P(EV, None, TILE),
    )
    return jax.shard_map(on_device, mesh=split, in_specs=placed, out_specs=P(EV, TILE), check_vma=False)
```

```python
import functools

import jax
import jax.numpy as jnp
import numpy as np
from jax import lax
from jax.experimental import pallas as pl
from jax.experimental.pallas import tpu as pltpu
from jax.sharding import Mesh
from jax.sharding import PartitionSpec as P

SWEEPS = 4
SMOOTH = 0.024

YS, ZS, CS, XS, WS = 4, 8, 2, 4, 2
EV, TILE = ("y", "z", "c"), "tile"
LISTS = XS * WS
TILE_FIRST, Y_FIRST, Z_FIRST = 5, 2, 4


def order(first, count):
    return [[first ^ i for i in range(count)]]


EVENTS, SLOTS, ROWS, COLS, LANES = 2, 256, 512, 256, 128
KERN = 64
SHARE = ROWS // (YS * ZS * CS)
PAD = 8
EDGE = 8
SPAN = COLS + 2 * EDGE
LINES = ROWS // LANES
BLOCK = 32


def pack(times, kernels, blocks, dests, counts, out):
    lane = lax.broadcasted_iota(jnp.int32, (1, LANES), 1)
    for e in range(EVENTS):
        for h in range(2):
            part = slice(h * LANES, (h + 1) * LANES)
            live = lane + h * LANES < counts[0, e]
            k = 2 * e + h
            out[0, k : k + 1, :] = times[0, e : e + 1, part]
            out[0, 4 + k : 5 + k, :] = jnp.where(live, kernels[0, e : e + 1, part], -1).astype(jnp.float32)
            out[0, 8 + k : 9 + k, :] = blocks[0, e : e + 1, part].astype(jnp.float32)
            out[0, 12 + k : 13 + k, :] = dests[e, :, part].astype(jnp.float32)
    for p in range(1, LISTS):
        out[p] = out[0]


def weight_columns(table):
    columns = jnp.transpose(table[...].astype(jnp.float32)) * (1.0 / 256.0)
    none = jnp.zeros((LANES, KERN), jnp.float32)
    return jnp.concatenate(
        [
            jnp.concatenate([columns[LANES - EDGE :]] + [none[:EDGE]] * 3, axis=1),
            jnp.concatenate([none, columns, none, none], axis=1),
            jnp.concatenate([none, none, columns, none], axis=1),
            jnp.concatenate([none[:EDGE]] * 3 + [columns[:EDGE]], axis=1),
        ],
        axis=0,
    ).astype(jnp.bfloat16)


def build(arrived, by_segment, tile, e, onehot, cells):
    f32, bf16 = jnp.float32, jnp.bfloat16
    pick = lax.broadcasted_iota(jnp.int32, (4 * KERN, SLOTS), 0)
    row_of = lax.broadcasted_iota(jnp.int32, (ROWS, SLOTS), 0)
    for t in range(LISTS):

        def both(k):
            k = k + 2 * e
            return jnp.concatenate([arrived[t, k : k + 1, :], arrived[t, k + 1 : k + 2, :]], axis=1)

        time = both(0)
        kernel = both(4).astype(jnp.int32)
        block = both(8).astype(jnp.int32)
        dest = both(12).astype(jnp.int32)
        seg = dest * 2 + (block & 1) - 2 * tile + 1
        row = block >> 1
        place = (row & (LINES - 1)) * LANES + row // LINES
        choice = jnp.where((kernel >= 0) & (seg >= 0) & (seg < 4), seg * KERN + kernel, -1)
        at = slice(t * SLOTS, (t + 1) * SLOTS)
        onehot[e, :, at] = jnp.where(row_of == place, 1.0, 0.0).astype(bf16)
        picked = jnp.where(pick == choice, 1.0, 0.0).astype(bf16)
        w = jnp.dot(by_segment, picked, preferred_element_type=f32)
        v = w * time
        v_hi = v.astype(bf16)
        cells[e, 0:SPAN, at] = w.astype(bf16)
        cells[e, SPAN : 2 * SPAN, at] = v_hi
        cells[e, 2 * SPAN : 3 * SPAN, at] = (v - v_hi.astype(f32)).astype(bf16)


def total(cells, onehot, e, r):
    sums = lax.dot_general(
        cells[e], onehot[e, r : r + 256], (((1,), (1,)), ((), ())), preferred_element_type=jnp.float32
    )
    return sums[0:SPAN], sums[SPAN : 2 * SPAN] + sums[2 * SPAN : 3 * SPAN]


def start(weight, number, e, r, keeps, adds, change):
    for t in range(r // LANES, r // LANES + 2):
        part = slice(t * LANES - r, (t + 1) * LANES - r)
        first = SMOOTH * number[:, part]
        keeps[e, t] = 1.0 - SMOOTH * weight[:, part]
        adds[e, t] = first
        change[e, t, PAD : PAD + SPAN, :] = first


def beside(tiles, lane):
    first = jnp.where(lane == 0, 0.0, pltpu.roll(tiles[-1], 1, 1))
    last = jnp.where(lane == LANES - 1, 0.0, pltpu.roll(tiles[0], LANES - 1, 1))
    return [first] + tiles[:-1], tiles[1:] + [last]


def laplace_of(buf, e, p, size, lane):
    near = [buf[e, t, PAD + p : PAD + p + size, :] for t in range(LINES)]
    above, below = beside(near, lane)
    out = []
    for t in range(LINES):
        left = buf[e, t, PAD + p - 1 : PAD + p - 1 + size, :]
        right = buf[e, t, PAD + p + 1 : PAD + p + 1 + size, :]
        out.append((left + right) + (above[t] + below[t]) - 4.0 * near[t])
    return out


def work(
    arrived, table, source_row, source_col, valid_hbm, send, keep,
    onehot, cells, keeps, adds, change, curve, valid, stacked, arrivals,
):
    f32 = jnp.float32
    tile = lax.axis_index("tile")
    core = lax.axis_index("c")
    copies = [
        pltpu.make_async_copy(
            valid_hbm.at[e, :, h * LANES : (h + 1) * LANES], valid.at[e, h], arrivals.at[2 * e + h]
        )
        for e in range(EVENTS)
        for h in range(2)
    ]
    for copy in copies:
        copy.start()
    empty = jnp.zeros((PAD, LANES), f32)
    for buf in (change, curve):
        for e in range(EVENTS):
            for t in range(LINES):
                buf[e, t, 0:PAD, :] = empty
                buf[e, t, PAD + SPAN :, :] = empty

    lane = lax.broadcasted_iota(jnp.int32, (1, LANES), 1)
    inside = {
        0: jnp.where(tile == 0, 0.0, 1.0).astype(f32),
        SPAN - EDGE: jnp.where(tile == LISTS - 1, 0.0, 1.0).astype(f32),
    }
    cuts = [0] + list(range(EDGE, SPAN - EDGE, BLOCK)) + [SPAN - EDGE, SPAN]
    parts = [(p, q - p) for p, q in zip(cuts, cuts[1:])]

    def sweep(e):
        for p, size in parts:
            for t, lap in enumerate(laplace_of(change, e, p, size, lane)):
                curve[e, t, PAD + p : PAD + p + size, :] = lap * inside[p] if p in inside else lap
        for p, size in parts:
            for t, bend in enumerate(laplace_of(curve, e, p, size, lane)):
                old = change[e, t, PAD + p : PAD + p + size, :]
                new = keeps[e, t, p : p + size, :] * old + (adds[e, t, p : p + size, :] - SMOOTH * bend)
                change[e, t, PAD + p : PAD + p + size, :] = new * inside[p] if p in inside else new

    lines = lax.broadcasted_iota(jnp.int32, (1, LANES), 1) * LINES
    column = lax.broadcasted_iota(jnp.int32, (LANES, 1), 0) + tile * COLS

    def stack(e):
        for h in range(2):
            p = PAD + EDGE + h * LANES
            near = [change[e, t, p : p + LANES, :] for t in range(LINES)]
            above, below = beside(near, lane)
            off_col = (column + h * LANES).astype(f32) - source_col[e]
            for t in range(LINES):
                left = change[e, t, p - 1 : p - 1 + LANES, :]
                right = change[e, t, p + 1 : p + 1 + LANES, :]
                off_row = (lines + t).astype(f32) - source_row[e]
                inverse = lax.rsqrt(off_row * off_row + off_col * off_col)
                along_row = off_row * inverse + 0.5 * (below[t] - above[t])
                along_col = off_col * inverse + 0.5 * (right - left)
                speed = jnp.sqrt(along_row * along_row + along_col * along_col)
                at = pl.ds(t, LANES, stride=LINES)
                term = valid[e, h, at, :] * jnp.transpose(speed)
                stacked[h, at, :] = term if e == 0 else stacked[h, at, :] + term

    by_segment = weight_columns(table)
    build(arrived, by_segment, tile, 0, onehot, cells)
    start(*total(cells, onehot, 0, 0), 0, 0, keeps, adds, change)
    build(arrived, by_segment, tile, 1, onehot, cells)
    start(*total(cells, onehot, 0, 256), 0, 256, keeps, adds, change)
    sweep(0)
    start(*total(cells, onehot, 1, 0), 1, 0, keeps, adds, change)
    sweep(0)
    start(*total(cells, onehot, 1, 256), 1, 256, keeps, adds, change)
    sweep(0)
    for copy in copies:
        copy.wait()
    stack(0)
    for k in range(SWEEPS - 1):
        sweep(1)
    stack(1)

    def deal(out, core_of):
        def one_share(g, carry):
            at = pl.ds(pl.multiple_of(g * (CS * SHARE) + core_of * SHARE, SHARE), SHARE)
            k = g ^ (Y_FIRST * ZS + Z_FIRST)
            for h in range(2):
                part = slice(h * LANES, (h + 1) * LANES)
                out[k, 0, :, part] = stacked[h, at, :]
                out[k, 1, :, part] = valid[0, h, at, :] + valid[1, h, at, :]
            return carry

        lax.fori_loop(0, YS * ZS, one_share, 0, unroll=8)

    deal(send, 1 - core)
    deal(keep, core)


def maps_of(arrived, table, source_row, source_col, valid):
    f32 = jnp.float32
    shares = jax.ShapeDtypeStruct((YS * ZS, 2, SHARE, COLS), f32)
    vmem, smem = pl.BlockSpec(memory_space=pltpu.VMEM), pl.BlockSpec(memory_space=pltpu.SMEM)
    wide = pltpu.VMEM((EVENTS, LINES, SPAN, LANES), f32)
    padded = pltpu.VMEM((EVENTS, LINES, SPAN + 2 * PAD, LANES), f32)
    return pl.pallas_call(
        work,
        out_shape=(shares, shares),
        in_specs=[vmem, vmem, smem, smem, pl.BlockSpec(memory_space=pltpu.HBM)],
        out_specs=(vmem, vmem),
        scratch_shapes=[
            pltpu.VMEM((EVENTS, ROWS, LISTS * SLOTS), jnp.bfloat16),
            pltpu.VMEM((EVENTS, 3 * SPAN, LISTS * SLOTS), jnp.bfloat16),
            wide, wide, padded, padded,
            pltpu.VMEM((EVENTS, 2, ROWS, LANES), f32),
            pltpu.VMEM((2, ROWS, LANES), f32),
            pltpu.SemaphoreType.DMA((2 * EVENTS,)),
        ],
        compiler_params=pltpu.CompilerParams(vmem_limit_bytes=53760 * 1024),
        name="maps",
    )(arrived, table, source_row, source_col, valid)


def packed(times, kernels, blocks, dests, counts):
    vmem, smem = pl.BlockSpec(memory_space=pltpu.VMEM), pl.BlockSpec(memory_space=pltpu.SMEM)
    return pl.pallas_call(
        pack,
        out_shape=jax.ShapeDtypeStruct((LISTS, 16, LANES), jnp.float32),
        in_specs=[vmem, vmem, vmem, vmem, smem],
        out_specs=vmem,
        name="pack",
    )(times, kernels, blocks, dests, counts)


def on_device(times, kernels, blocks, dests, counts, table, source_row, source_col, valid):
    outgoing = packed(times, kernels, blocks, dests.reshape(EVENTS, 1, SLOTS), counts)
    arrived = lax.all_to_all(outgoing, TILE, 0, 0, tiled=True, axis_index_groups=order(TILE_FIRST, LISTS))
    send, keep = maps_of(arrived, table, source_row, source_col, valid)
    both = keep + lax.ppermute(send, "c", [(0, 1), (1, 0)])
    both = both.reshape(YS, ZS, 2, SHARE, COLS)
    both = jnp.sum(lax.all_to_all(both, "y", 0, 0, tiled=True, axis_index_groups=order(Y_FIRST, YS)), axis=0)
    both = jnp.sum(lax.all_to_all(both, "z", 0, 0, tiled=True, axis_index_groups=order(Z_FIRST, ZS)), axis=0)
    return both[0] / (1.0 + both[1])


def solution(mesh):
    split = Mesh(np.asarray(mesh.devices).reshape(YS, ZS, CS, XS * WS), EV + (TILE,))
    placed = (
        P(TILE, EV, None),
        P(TILE, EV, None),
        P(TILE, EV, None),
        P(TILE, EV, None, None),
        P(TILE, EV),
        P(),
        P(EV),
        P(EV),
        P(EV, None, TILE),
    )
    return jax.shard_map(on_device, mesh=split, in_specs=placed, out_specs=P(EV, TILE), check_vma=False)
```

```python
import functools

import jax
import jax.numpy as jnp
import numpy as np
from jax import lax
from jax.experimental import pallas as pl
from jax.experimental.pallas import tpu as pltpu
from jax.sharding import Mesh
from jax.sharding import PartitionSpec as P

SWEEPS = 4
SMOOTH = 0.024

YS, ZS, CS, XS, WS = 4, 8, 2, 4, 2
EV, TILE = ("y", "z", "c"), "tile"
LISTS = XS * WS
TILE_FIRST, Y_FIRST, Z_FIRST = 5, 2, 4


def order(first, count):
    return [[first ^ i for i in range(count)]]


EVENTS, SLOTS, ROWS, COLS, LANES = 2, 256, 512, 256, 128
KERN = 64
SHARE = ROWS // (YS * ZS * CS)
PAD = 8
EDGE = 8
SPAN = COLS + 2 * EDGE
LINES = ROWS // LANES
BLOCK = 32


def pack(times, kernels, blocks, dests, counts, out):
    lane = lax.broadcasted_iota(jnp.int32, (1, LANES), 1)
    for e in range(EVENTS):
        for h in range(2):
            part = slice(h * LANES, (h + 1) * LANES)
            live = lane + h * LANES < counts[0, e]
            k = 2 * e + h
            out[0, k : k + 1, :] = times[0, e : e + 1, part]
            out[0, 4 + k : 5 + k, :] = jnp.where(live, kernels[0, e : e + 1, part], -1).astype(jnp.float32)
            out[0, 8 + k : 9 + k, :] = blocks[0, e : e + 1, part].astype(jnp.float32)
            out[0, 12 + k : 13 + k, :] = dests[e, :, part].astype(jnp.float32)
    for p in range(1, LISTS):
        out[p] = out[0]


def weight_columns(table):
    columns = jnp.transpose(table[...].astype(jnp.float32)) * (1.0 / 256.0)
    none = jnp.zeros((LANES, KERN), jnp.float32)
    return jnp.concatenate(
        [
            jnp.concatenate([columns[LANES - EDGE :]] + [none[:EDGE]] * 3, axis=1),
            jnp.concatenate([none, columns, none, none], axis=1),
            jnp.concatenate([none, none, columns, none], axis=1),
            jnp.concatenate([none[:EDGE]] * 3 + [columns[:EDGE]], axis=1),
        ],
        axis=0,
    ).astype(jnp.bfloat16)


def build(arrived, by_segment, tile, e, onehot, cells):
    f32, bf16 = jnp.float32, jnp.bfloat16
    pick = lax.broadcasted_iota(jnp.int16, (4 * KERN, SLOTS), 0)
    row_of = lax.broadcasted_iota(jnp.int16, (ROWS, SLOTS), 0)
    for t in range(LISTS):

        def both(k):
            k = k + 2 * e
            return jnp.concatenate([arrived[t, k : k + 1, :], arrived[t, k + 1 : k + 2, :]], axis=1)

        time = both(0)
        kernel = both(4).astype(jnp.int32)
        block = both(8).astype(jnp.int32)
        dest = both(12).astype(jnp.int32)
        seg = dest * 2 + (block & 1) - 2 * tile + 1
        row = block >> 1
        place = (row & (LINES - 1)) * LANES + row // LINES
        choice = jnp.where((kernel >= 0) & (seg >= 0) & (seg < 4), seg * KERN + kernel, -1)
        at = slice(t * SLOTS, (t + 1) * SLOTS)
        onehot[e, :, at] = jnp.where(row_of == place.astype(jnp.int16), bf16(1), bf16(0))
        picked = jnp.where(pick == choice.astype(jnp.int16), bf16(1), bf16(0))
        w = jnp.dot(by_segment, picked, preferred_element_type=f32)
        v = w * time
        v_hi = v.astype(bf16)
        cells[e, 0:SPAN, at] = w.astype(bf16)
        cells[e, SPAN : 2 * SPAN, at] = v_hi
        cells[e, 2 * SPAN : 3 * SPAN, at] = (v - v_hi.astype(f32)).astype(bf16)


def total(cells, onehot, e, r):
    sums = lax.dot_general(
        cells[e], onehot[e, r : r + 256], (((1,), (1,)), ((), ())), preferred_element_type=jnp.float32
    )
    return sums[0:SPAN], sums[SPAN : 2 * SPAN] + sums[2 * SPAN : 3 * SPAN]


def start(weight, number, e, r, keeps, adds, change):
    for t in range(r // LANES, r // LANES + 2):
        part = slice(t * LANES - r, (t + 1) * LANES - r)
        first = SMOOTH * number[:, part]
        keeps[e, t] = 1.0 - SMOOTH * weight[:, part]
        adds[e, t] = first
        change[e, t, PAD : PAD + SPAN, :] = first


def beside(tiles, lane):
    first = jnp.where(lane == 0, 0.0, pltpu.roll(tiles[-1], 1, 1))
    last = jnp.where(lane == LANES - 1, 0.0, pltpu.roll(tiles[0], LANES - 1, 1))
    return [first] + tiles[:-1], tiles[1:] + [last]


def laplace_of(buf, e, p, size, lane):
    near = [buf[e, t, PAD + p : PAD + p + size, :] for t in range(LINES)]
    above, below = beside(near, lane)
    out = []
    for t in range(LINES):
        left = buf[e, t, PAD + p - 1 : PAD + p - 1 + size, :]
        right = buf[e, t, PAD + p + 1 : PAD + p + 1 + size, :]
        out.append((left + right) + (above[t] + below[t]) - 4.0 * near[t])
    return out


def work(
    arrived, table, source_row, source_col, valid_hbm, send, keep,
    onehot, cells, keeps, adds, change, curve, valid, stacked, arrivals,
):
    f32 = jnp.float32
    tile = lax.axis_index("tile")
    core = lax.axis_index("c")
    copies = [
        pltpu.make_async_copy(
            valid_hbm.at[e, :, h * LANES : (h + 1) * LANES], valid.at[e, h], arrivals.at[2 * e + h]
        )
        for e in range(EVENTS)
        for h in range(2)
    ]
    for copy in copies:
        copy.start()
    empty = jnp.zeros((PAD, LANES), f32)
    for buf in (change, curve):
        for e in range(EVENTS):
            for t in range(LINES):
                buf[e, t, 0:PAD, :] = empty
                buf[e, t, PAD + SPAN :, :] = empty

    lane = lax.broadcasted_iota(jnp.int32, (1, LANES), 1)
    inside = {
        0: jnp.where(tile == 0, 0.0, 1.0).astype(f32),
        SPAN - EDGE: jnp.where(tile == LISTS - 1, 0.0, 1.0).astype(f32),
    }
    cuts = [0] + list(range(EDGE, SPAN - EDGE, BLOCK)) + [SPAN - EDGE, SPAN]
    parts = [(p, q - p) for p, q in zip(cuts, cuts[1:])]

    def sweep(e):
        for p, size in parts:
            for t, lap in enumerate(laplace_of(change, e, p, size, lane)):
                curve[e, t, PAD + p : PAD + p + size, :] = lap * inside[p] if p in inside else lap
        for p, size in parts:
            for t, bend in enumerate(laplace_of(curve, e, p, size, lane)):
                old = change[e, t, PAD + p : PAD + p + size, :]
                new = keeps[e, t, p : p + size, :] * old + (adds[e, t, p : p + size, :] - SMOOTH * bend)
                change[e, t, PAD + p : PAD + p + size, :] = new * inside[p] if p in inside else new

    lines = lax.broadcasted_iota(jnp.int32, (1, LANES), 1) * LINES
    column = lax.broadcasted_iota(jnp.int32, (LANES, 1), 0) + tile * COLS

    def stack(e):
        for h in range(2):
            p = PAD + EDGE + h * LANES
            near = [change[e, t, p : p + LANES, :] for t in range(LINES)]
            above, below = beside(near, lane)
            off_col = (column + h * LANES).astype(f32) - source_col[e]
            for t in range(LINES):
                left = change[e, t, p - 1 : p - 1 + LANES, :]
                right = change[e, t, p + 1 : p + 1 + LANES, :]
                off_row = (lines + t).astype(f32) - source_row[e]
                inverse = lax.rsqrt(off_row * off_row + off_col * off_col)
                along_row = off_row * inverse + 0.5 * (below[t] - above[t])
                along_col = off_col * inverse + 0.5 * (right - left)
                speed = jnp.sqrt(along_row * along_row + along_col * along_col)
                at = pl.ds(t, LANES, stride=LINES)
                term = valid[e, h, at, :] * jnp.transpose(speed)
                stacked[h, at, :] = term if e == 0 else stacked[h, at, :] + term

    by_segment = weight_columns(table)
    build(arrived, by_segment, tile, 0, onehot, cells)
    start(*total(cells, onehot, 0, 0), 0, 0, keeps, adds, change)
    build(arrived, by_segment, tile, 1, onehot, cells)
    start(*total(cells, onehot, 0, 256), 0, 256, keeps, adds, change)
    sweep(0)
    start(*total(cells, onehot, 1, 0), 1, 0, keeps, adds, change)
    sweep(0)
    start(*total(cells, onehot, 1, 256), 1, 256, keeps, adds, change)
    sweep(0)
    for copy in copies:
        copy.wait()
    stack(0)
    for k in range(SWEEPS - 1):
        sweep(1)
    stack(1)

    def deal(out, core_of):
        first = pl.multiple_of(core_of * SHARE, SHARE)
        for g in range(YS * ZS):
            at = pl.ds(first + g * (CS * SHARE), SHARE)
            k = g ^ (Y_FIRST * ZS + Z_FIRST)
            for h in range(2):
                part = slice(h * LANES, (h + 1) * LANES)
                out[k, 0, :, part] = stacked[h, at, :]
                out[k, 1, :, part] = valid[0, h, at, :] + valid[1, h, at, :]

    deal(send, 1 - core)
    deal(keep, core)


def maps_of(arrived, table, source_row, source_col, valid):
    f32 = jnp.float32
    shares = jax.ShapeDtypeStruct((YS * ZS, 2, SHARE, COLS), f32)
    vmem, smem = pl.BlockSpec(memory_space=pltpu.VMEM), pl.BlockSpec(memory_space=pltpu.SMEM)
    wide = pltpu.VMEM((EVENTS, LINES, SPAN, LANES), f32)
    padded = pltpu.VMEM((EVENTS, LINES, SPAN + 2 * PAD, LANES), f32)
    return pl.pallas_call(
        work,
        out_shape=(shares, shares),
        in_specs=[vmem, vmem, smem, smem, pl.BlockSpec(memory_space=pltpu.HBM)],
        out_specs=(vmem, vmem),
        scratch_shapes=[
            pltpu.VMEM((EVENTS, ROWS, LISTS * SLOTS), jnp.bfloat16),
            pltpu.VMEM((EVENTS, 3 * SPAN, LISTS * SLOTS), jnp.bfloat16),
            wide, wide, padded, padded,
            pltpu.VMEM((EVENTS, 2, ROWS, LANES), f32),
            pltpu.VMEM((2, ROWS, LANES), f32),
            pltpu.SemaphoreType.DMA((2 * EVENTS,)),
        ],
        compiler_params=pltpu.CompilerParams(vmem_limit_bytes=53760 * 1024),
        name="maps",
    )(arrived, table, source_row, source_col, valid)


def packed(times, kernels, blocks, dests, counts):
    vmem, smem = pl.BlockSpec(memory_space=pltpu.VMEM), pl.BlockSpec(memory_space=pltpu.SMEM)
    return pl.pallas_call(
        pack,
        out_shape=jax.ShapeDtypeStruct((LISTS, 16, LANES), jnp.float32),
        in_specs=[vmem, vmem, vmem, vmem, smem],
        out_specs=vmem,
        name="pack",
    )(times, kernels, blocks, dests, counts)


def on_device(times, kernels, blocks, dests, counts, table, source_row, source_col, valid):
    outgoing = packed(times, kernels, blocks, dests.reshape(EVENTS, 1, SLOTS), counts)
    arrived = lax.all_to_all(outgoing, TILE, 0, 0, tiled=True, axis_index_groups=order(TILE_FIRST, LISTS))
    send, keep = maps_of(arrived, table, source_row, source_col, valid)
    both = keep + lax.ppermute(send, "c", [(0, 1), (1, 0)])
    both = both.reshape(YS, ZS, 2, SHARE, COLS)
    both = jnp.sum(lax.all_to_all(both, "y", 0, 0, tiled=True, axis_index_groups=order(Y_FIRST, YS)), axis=0)
    both = jnp.sum(lax.all_to_all(both, "z", 0, 0, tiled=True, axis_index_groups=order(Z_FIRST, ZS)), axis=0)
    return both[0] / (1.0 + both[1])


def solution(mesh):
    split = Mesh(np.asarray(mesh.devices).reshape(YS, ZS, CS, XS * WS), EV + (TILE,))
    placed = (
        P(TILE, EV, None),
        P(TILE, EV, None),
        P(TILE, EV, None),
        P(TILE, EV, None, None),
        P(TILE, EV),
        P(),
        P(EV),
        P(EV),
        P(EV, None, TILE),
    )
    return jax.shard_map(on_device, mesh=split, in_specs=placed, out_specs=P(EV, TILE), check_vma=False)
```

```python
import functools

import jax
import jax.numpy as jnp
import numpy as np
from jax import lax
from jax.experimental import pallas as pl
from jax.experimental.pallas import tpu as pltpu
from jax.sharding import Mesh
from jax.sharding import PartitionSpec as P

SWEEPS = 4
SMOOTH = 0.024

YS, ZS, CS, XS, WS = 4, 8, 2, 4, 2
EV, TILE = ("y", "z", "c"), "tile"
LISTS = XS * WS
TILE_FIRST, Y_FIRST, Z_FIRST = 5, 2, 4


def order(first, count):
    return [[first ^ i for i in range(count)]]


EVENTS, SLOTS, ROWS, COLS, LANES = 2, 256, 512, 256, 128
KERN = 64
SHARE = ROWS // (YS * ZS * CS)
PAD = 8
EDGE = 8
SPAN = COLS + 2 * EDGE
LINES = ROWS // LANES
BLOCK = 32


def pack(times, kernels, blocks, dests, counts, out):
    lane = lax.broadcasted_iota(jnp.int32, (1, LANES), 1)
    for e in range(EVENTS):
        for h in range(2):
            part = slice(h * LANES, (h + 1) * LANES)
            live = lane + h * LANES < counts[0, e]
            k = 2 * e + h
            out[0, k : k + 1, :] = times[0, e : e + 1, part]
            out[0, 4 + k : 5 + k, :] = jnp.where(live, kernels[0, e : e + 1, part], -1).astype(jnp.float32)
            out[0, 8 + k : 9 + k, :] = blocks[0, e : e + 1, part].astype(jnp.float32)
            out[0, 12 + k : 13 + k, :] = dests[e, :, part].astype(jnp.float32)
    for p in range(1, LISTS):
        out[p] = out[0]


def weight_columns(table):
    columns = jnp.transpose(table[...].astype(jnp.float32)) * (1.0 / 256.0)
    none = jnp.zeros((LANES, KERN), jnp.float32)
    return jnp.concatenate(
        [
            jnp.concatenate([columns[LANES - EDGE :]] + [none[:EDGE]] * 3, axis=1),
            jnp.concatenate([none, columns, none, none], axis=1),
            jnp.concatenate([none, none, columns, none], axis=1),
            jnp.concatenate([none[:EDGE]] * 3 + [columns[:EDGE]], axis=1),
        ],
        axis=0,
    ).astype(jnp.bfloat16)


def build(arrived, by_segment, tile, e, onehot, cells):
    f32, bf16 = jnp.float32, jnp.bfloat16
    pick = lax.broadcasted_iota(jnp.int16, (4 * KERN, SLOTS), 0)
    row_of = lax.broadcasted_iota(jnp.int16, (ROWS, SLOTS), 0)
    rows = [arrived[t] for t in range(LISTS)]
    choices, times = [], []
    for t in range(LISTS):

        def both(k):
            k = k + 2 * e
            return jnp.concatenate([rows[t][k : k + 1, :], rows[t][k + 1 : k + 2, :]], axis=1)

        time = both(0)
        kernel = both(4).astype(jnp.int32)
        block = both(8).astype(jnp.int32)
        dest = both(12).astype(jnp.int32)
        seg = dest * 2 + (block & 1) - 2 * tile + 1
        row = block >> 1
        place = (row & (LINES - 1)) * LANES + row // LINES
        choice = jnp.where((kernel >= 0) & (seg >= 0) & (seg < 4), seg * KERN + kernel, -1)
        at = slice(t * SLOTS, (t + 1) * SLOTS)
        onehot[e, :, at] = jnp.where(row_of == place.astype(jnp.int16), bf16(1), bf16(0))
        choices.append(choice.astype(jnp.int16))
        times.append(time)
    for t in range(0, LISTS, 2):
        at = slice(t * SLOTS, (t + 2) * SLOTS)
        picked = jnp.concatenate([jnp.where(pick == c, bf16(1), bf16(0)) for c in choices[t : t + 2]], axis=1)
        w = jnp.dot(by_segment, picked, preferred_element_type=f32)
        v = w * jnp.concatenate(times[t : t + 2], axis=1)
        v_hi = v.astype(bf16)
        cells[e, 0:SPAN, at] = w.astype(bf16)
        cells[e, SPAN : 2 * SPAN, at] = v_hi
        cells[e, 2 * SPAN : 3 * SPAN, at] = (v - v_hi.astype(f32)).astype(bf16)


def total(cells, onehot, e, r):
    sums = lax.dot_general(
        cells[e], onehot[e, r : r + 256], (((1,), (1,)), ((), ())), preferred_element_type=jnp.float32
    )
    return sums[0:SPAN], sums[SPAN : 2 * SPAN] + sums[2 * SPAN : 3 * SPAN]


def start(weight, number, e, r, keeps, adds, change):
    for t in range(r // LANES, r // LANES + 2):
        part = slice(t * LANES - r, (t + 1) * LANES - r)
        first = SMOOTH * number[:, part]
        keeps[e, t] = 1.0 - SMOOTH * weight[:, part]
        adds[e, t] = first
        change[e, t, PAD : PAD + SPAN, :] = first


def beside(tiles, lane):
    first = jnp.where(lane == 0, 0.0, pltpu.roll(tiles[-1], 1, 1))
    last = jnp.where(lane == LANES - 1, 0.0, pltpu.roll(tiles[0], LANES - 1, 1))
    return [first] + tiles[:-1], tiles[1:] + [last]


def laplace_of(buf, e, p, size, lane):
    near = [buf[e, t, PAD + p : PAD + p + size, :] for t in range(LINES)]
    above, below = beside(near, lane)
    out = []
    for t in range(LINES):
        left = buf[e, t, PAD + p - 1 : PAD + p - 1 + size, :]
        right = buf[e, t, PAD + p + 1 : PAD + p + 1 + size, :]
        out.append((left + right) + (above[t] + below[t]) - 4.0 * near[t])
    return out


def work(
    arrived, table, source_row, source_col, valid_hbm, send, keep,
    onehot, cells, keeps, adds, change, curve, valid, stacked, arrivals,
):
    f32 = jnp.float32
    tile = lax.axis_index("tile")
    core = lax.axis_index("c")
    copies = [
        pltpu.make_async_copy(
            valid_hbm.at[e, :, h * LANES : (h + 1) * LANES], valid.at[e, h], arrivals.at[2 * e + h]
        )
        for e in range(EVENTS)
        for h in range(2)
    ]
    for copy in copies:
        copy.start()
    empty = jnp.zeros((PAD, LANES), f32)
    for buf in (change, curve):
        for e in range(EVENTS):
            for t in range(LINES):
                buf[e, t, 0:PAD, :] = empty
                buf[e, t, PAD + SPAN :, :] = empty

    lane = lax.broadcasted_iota(jnp.int32, (1, LANES), 1)
    inside = {
        0: jnp.where(tile == 0, 0.0, 1.0).astype(f32),
        SPAN - EDGE: jnp.where(tile == LISTS - 1, 0.0, 1.0).astype(f32),
    }
    cuts = [0] + list(range(EDGE, SPAN - EDGE, BLOCK)) + [SPAN - EDGE, SPAN]
    parts = [(p, q - p) for p, q in zip(cuts, cuts[1:])]

    def sweep(e):
        for p, size in parts:
            for t, lap in enumerate(laplace_of(change, e, p, size, lane)):
                curve[e, t, PAD + p : PAD + p + size, :] = lap * inside[p] if p in inside else lap
        for p, size in parts:
            for t, bend in enumerate(laplace_of(curve, e, p, size, lane)):
                old = change[e, t, PAD + p : PAD + p + size, :]
                new = keeps[e, t, p : p + size, :] * old + (adds[e, t, p : p + size, :] - SMOOTH * bend)
                change[e, t, PAD + p : PAD + p + size, :] = new * inside[p] if p in inside else new

    lines = lax.broadcasted_iota(jnp.int32, (1, LANES), 1) * LINES
    column = lax.broadcasted_iota(jnp.int32, (LANES, 1), 0) + tile * COLS

    def stack(e):
        for h in range(2):
            p = PAD + EDGE + h * LANES
            near = [change[e, t, p : p + LANES, :] for t in range(LINES)]
            above, below = beside(near, lane)
            off_col = (column + h * LANES).astype(f32) - source_col[e]
            for t in range(LINES):
                left = change[e, t, p - 1 : p - 1 + LANES, :]
                right = change[e, t, p + 1 : p + 1 + LANES, :]
                off_row = (lines + t).astype(f32) - source_row[e]
                inverse = lax.rsqrt(off_row * off_row + off_col * off_col)
                along_row = off_row * inverse + 0.5 * (below[t] - above[t])
                along_col = off_col * inverse + 0.5 * (right - left)
                speed = jnp.sqrt(along_row * along_row + along_col * along_col)
                at = pl.ds(t, LANES, stride=LINES)
                term = valid[e, h, at, :] * jnp.transpose(speed)
                stacked[h, at, :] = term if e == 0 else stacked[h, at, :] + term

    by_segment = weight_columns(table)
    build(arrived, by_segment, tile, 0, onehot, cells)
    start(*total(cells, onehot, 0, 0), 0, 0, keeps, adds, change)
    build(arrived, by_segment, tile, 1, onehot, cells)
    start(*total(cells, onehot, 0, 256), 0, 256, keeps, adds, change)
    sweep(0)
    start(*total(cells, onehot, 1, 0), 1, 0, keeps, adds, change)
    sweep(0)
    start(*total(cells, onehot, 1, 256), 1, 256, keeps, adds, change)
    sweep(0)
    for copy in copies:
        copy.wait()
    stack(0)
    for k in range(SWEEPS - 1):
        sweep(1)
    stack(1)

    def deal(out, core_of):
        first = pl.multiple_of(core_of * SHARE, SHARE)
        for g in range(YS * ZS):
            at = pl.ds(first + g * (CS * SHARE), SHARE)
            k = g ^ (Y_FIRST * ZS + Z_FIRST)
            for h in range(2):
                part = slice(h * LANES, (h + 1) * LANES)
                out[k, 0, :, part] = stacked[h, at, :]
                out[k, 1, :, part] = valid[0, h, at, :] + valid[1, h, at, :]

    deal(send, 1 - core)
    deal(keep, core)


def maps_of(arrived, table, source_row, source_col, valid):
    f32 = jnp.float32
    shares = jax.ShapeDtypeStruct((YS * ZS, 2, SHARE, COLS), f32)
    vmem, smem = pl.BlockSpec(memory_space=pltpu.VMEM), pl.BlockSpec(memory_space=pltpu.SMEM)
    wide = pltpu.VMEM((EVENTS, LINES, SPAN, LANES), f32)
    padded = pltpu.VMEM((EVENTS, LINES, SPAN + 2 * PAD, LANES), f32)
    return pl.pallas_call(
        work,
        out_shape=(shares, shares),
        in_specs=[vmem, vmem, smem, smem, pl.BlockSpec(memory_space=pltpu.HBM)],
        out_specs=(vmem, vmem),
        scratch_shapes=[
            pltpu.VMEM((EVENTS, ROWS, LISTS * SLOTS), jnp.bfloat16),
            pltpu.VMEM((EVENTS, 3 * SPAN, LISTS * SLOTS), jnp.bfloat16),
            wide, wide, padded, padded,
            pltpu.VMEM((EVENTS, 2, ROWS, LANES), f32),
            pltpu.VMEM((2, ROWS, LANES), f32),
            pltpu.SemaphoreType.DMA((2 * EVENTS,)),
        ],
        compiler_params=pltpu.CompilerParams(vmem_limit_bytes=53760 * 1024),
        name="maps",
    )(arrived, table, source_row, source_col, valid)


def packed(times, kernels, blocks, dests, counts):
    vmem, smem = pl.BlockSpec(memory_space=pltpu.VMEM), pl.BlockSpec(memory_space=pltpu.SMEM)
    return pl.pallas_call(
        pack,
        out_shape=jax.ShapeDtypeStruct((LISTS, 16, LANES), jnp.float32),
        in_specs=[vmem, vmem, vmem, vmem, smem],
        out_specs=vmem,
        name="pack",
    )(times, kernels, blocks, dests, counts)


def on_device(times, kernels, blocks, dests, counts, table, source_row, source_col, valid):
    outgoing = packed(times, kernels, blocks, dests.reshape(EVENTS, 1, SLOTS), counts)
    arrived = lax.all_to_all(outgoing, TILE, 0, 0, tiled=True, axis_index_groups=order(TILE_FIRST, LISTS))
    send, keep = maps_of(arrived, table, source_row, source_col, valid)
    both = keep + lax.ppermute(send, "c", [(0, 1), (1, 0)])
    both = both.reshape(YS, ZS, 2, SHARE, COLS)
    both = jnp.sum(lax.all_to_all(both, "y", 0, 0, tiled=True, axis_index_groups=order(Y_FIRST, YS)), axis=0)
    both = jnp.sum(lax.all_to_all(both, "z", 0, 0, tiled=True, axis_index_groups=order(Z_FIRST, ZS)), axis=0)
    return both[0] / (1.0 + both[1])


def solution(mesh):
    split = Mesh(np.asarray(mesh.devices).reshape(YS, ZS, CS, XS * WS), EV + (TILE,))
    placed = (
        P(TILE, EV, None),
        P(TILE, EV, None),
        P(TILE, EV, None),
        P(TILE, EV, None, None),
        P(TILE, EV),
        P(),
        P(EV),
        P(EV),
        P(EV, None, TILE),
    )
    return jax.shard_map(on_device, mesh=split, in_specs=placed, out_specs=P(EV, TILE), check_vma=False)
```

```python
import functools

import jax
import jax.numpy as jnp
import numpy as np
from jax import lax
from jax.experimental import pallas as pl
from jax.experimental.pallas import tpu as pltpu
from jax.sharding import Mesh
from jax.sharding import PartitionSpec as P

SWEEPS = 4
SMOOTH = 0.024

YS, ZS, CS, XS, WS = 4, 8, 2, 4, 2
EV, TILE = ("y", "z", "c"), "tile"
LISTS = XS * WS
TILE_FIRST, Y_FIRST, Z_FIRST = 5, 2, 4


def order(first, count):
    return [[first ^ i for i in range(count)]]


EVENTS, SLOTS, ROWS, COLS, LANES = 2, 256, 512, 256, 128
KERN = 64
SHARE = ROWS // (YS * ZS * CS)
PAD = 8
EDGE = 8
SPAN = COLS + 2 * EDGE
LINES = ROWS // LANES
BLOCK = 128


def pack(times, kernels, blocks, dests, counts, out):
    lane = lax.broadcasted_iota(jnp.int32, (1, LANES), 1)
    for e in range(EVENTS):
        for h in range(2):
            part = slice(h * LANES, (h + 1) * LANES)
            live = lane + h * LANES < counts[0, e]
            k = 2 * e + h
            out[0, k : k + 1, :] = times[0, e : e + 1, part]
            out[0, 4 + k : 5 + k, :] = jnp.where(live, kernels[0, e : e + 1, part], -1).astype(jnp.float32)
            out[0, 8 + k : 9 + k, :] = blocks[0, e : e + 1, part].astype(jnp.float32)
            out[0, 12 + k : 13 + k, :] = dests[e, :, part].astype(jnp.float32)
    for p in range(1, LISTS):
        out[p] = out[0]


def weight_columns(table):
    columns = jnp.transpose(table[...].astype(jnp.float32)) * (1.0 / 256.0)
    none = jnp.zeros((LANES, KERN), jnp.float32)
    return jnp.concatenate(
        [
            jnp.concatenate([columns[LANES - EDGE :]] + [none[:EDGE]] * 3, axis=1),
            jnp.concatenate([none, columns, none, none], axis=1),
            jnp.concatenate([none, none, columns, none], axis=1),
            jnp.concatenate([none[:EDGE]] * 3 + [columns[:EDGE]], axis=1),
        ],
        axis=0,
    ).astype(jnp.bfloat16)


def build(arrived, by_segment, tile, e, onehot, cells):
    f32, bf16 = jnp.float32, jnp.bfloat16
    pick = lax.broadcasted_iota(jnp.int16, (4 * KERN, SLOTS), 0)
    row_of = lax.broadcasted_iota(jnp.int16, (ROWS, SLOTS), 0)
    rows = [arrived[t] for t in range(LISTS)]
    choices, times = [], []
    for t in range(LISTS):

        def both(k):
            k = k + 2 * e
            return jnp.concatenate([rows[t][k : k + 1, :], rows[t][k + 1 : k + 2, :]], axis=1)

        time = both(0)
        kernel = both(4).astype(jnp.int32)
        block = both(8).astype(jnp.int32)
        dest = both(12).astype(jnp.int32)
        seg = dest * 2 + (block & 1) - 2 * tile + 1
        row = block >> 1
        place = (row & (LINES - 1)) * LANES + row // LINES
        choice = jnp.where((kernel >= 0) & (seg >= 0) & (seg < 4), seg * KERN + kernel, -1)
        at = slice(t * SLOTS, (t + 1) * SLOTS)
        onehot[e, :, at] = jnp.where(row_of == place.astype(jnp.int16), bf16(1), bf16(0))
        choices.append(choice.astype(jnp.int16))
        times.append(time)
    for t in range(0, LISTS, 4):
        at = slice(t * SLOTS, (t + 4) * SLOTS)
        picked = jnp.concatenate([jnp.where(pick == c, bf16(1), bf16(0)) for c in choices[t : t + 4]], axis=1)
        w = jnp.dot(by_segment, picked, preferred_element_type=f32)
        v = w * jnp.concatenate(times[t : t + 4], axis=1)
        v_hi = v.astype(bf16)
        cells[e, 0:SPAN, at] = w.astype(bf16)
        cells[e, SPAN : 2 * SPAN, at] = v_hi
        cells[e, 2 * SPAN : 3 * SPAN, at] = (v - v_hi.astype(f32)).astype(bf16)


def total(cells, onehot, e, r):
    sums = lax.dot_general(
        cells[e], onehot[e, r : r + 256], (((1,), (1,)), ((), ())), preferred_element_type=jnp.float32
    )
    return sums[0:SPAN], sums[SPAN : 2 * SPAN] + sums[2 * SPAN : 3 * SPAN]


def start(weight, number, e, r, keeps, adds, change):
    for t in range(r // LANES, r // LANES + 2):
        part = slice(t * LANES - r, (t + 1) * LANES - r)
        first = SMOOTH * number[:, part]
        keeps[e, t] = 1.0 - SMOOTH * weight[:, part]
        adds[e, t] = first
        change[e, t, PAD : PAD + SPAN, :] = first


def beside(tiles, lane):
    first = jnp.where(lane == 0, 0.0, pltpu.roll(tiles[-1], 1, 1))
    last = jnp.where(lane == LANES - 1, 0.0, pltpu.roll(tiles[0], LANES - 1, 1))
    return [first] + tiles[:-1], tiles[1:] + [last]


def laplace_of(buf, e, p, size, lane):
    near = [buf[e, t, PAD + p : PAD + p + size, :] for t in range(LINES)]
    above, below = beside(near, lane)
    out = []
    for t in range(LINES):
        left = buf[e, t, PAD + p - 1 : PAD + p - 1 + size, :]
        right = buf[e, t, PAD + p + 1 : PAD + p + 1 + size, :]
        out.append((left + right) + (above[t] + below[t]) - 4.0 * near[t])
    return out


def work(
    arrived, table, source_row, source_col, valid_hbm, send, keep,
    onehot, cells, keeps, adds, change, curve, valid, stacked, arrivals,
):
    f32 = jnp.float32
    tile = lax.axis_index("tile")
    core = lax.axis_index("c")
    copies = [
        pltpu.make_async_copy(
            valid_hbm.at[e, :, h * LANES : (h + 1) * LANES], valid.at[e, h], arrivals.at[2 * e + h]
        )
        for e in range(EVENTS)
        for h in range(2)
    ]
    for copy in copies:
        copy.start()
    empty = jnp.zeros((PAD, LANES), f32)
    for buf in (change, curve):
        for e in range(EVENTS):
            for t in range(LINES):
                buf[e, t, 0:PAD, :] = empty
                buf[e, t, PAD + SPAN :, :] = empty

    lane = lax.broadcasted_iota(jnp.int32, (1, LANES), 1)
    inside = {
        0: jnp.where(tile == 0, 0.0, 1.0).astype(f32),
        SPAN - EDGE: jnp.where(tile == LISTS - 1, 0.0, 1.0).astype(f32),
    }
    cuts = [0] + list(range(EDGE, SPAN - EDGE, BLOCK)) + [SPAN - EDGE, SPAN]
    parts = [(p, q - p) for p, q in zip(cuts, cuts[1:])]

    def sweep(e):
        for p, size in parts:
            for t, lap in enumerate(laplace_of(change, e, p, size, lane)):
                curve[e, t, PAD + p : PAD + p + size, :] = lap * inside[p] if p in inside else lap
        for p, size in parts:
            for t, bend in enumerate(laplace_of(curve, e, p, size, lane)):
                old = change[e, t, PAD + p : PAD + p + size, :]
                new = keeps[e, t, p : p + size, :] * old + (adds[e, t, p : p + size, :] - SMOOTH * bend)
                change[e, t, PAD + p : PAD + p + size, :] = new * inside[p] if p in inside else new

    lines = lax.broadcasted_iota(jnp.int32, (1, LANES), 1) * LINES
    column = lax.broadcasted_iota(jnp.int32, (LANES, 1), 0) + tile * COLS

    def stack(e):
        for h in range(2):
            p = PAD + EDGE + h * LANES
            near = [change[e, t, p : p + LANES, :] for t in range(LINES)]
            above, below = beside(near, lane)
            off_col = (column + h * LANES).astype(f32) - source_col[e]
            for t in range(LINES):
                left = change[e, t, p - 1 : p - 1 + LANES, :]
                right = change[e, t, p + 1 : p + 1 + LANES, :]
                off_row = (lines + t).astype(f32) - source_row[e]
                inverse = lax.rsqrt(off_row * off_row + off_col * off_col)
                along_row = off_row * inverse + 0.5 * (below[t] - above[t])
                along_col = off_col * inverse + 0.5 * (right - left)
                speed = jnp.sqrt(along_row * along_row + along_col * along_col)
                at = pl.ds(t, LANES, stride=LINES)
                term = valid[e, h, at, :] * jnp.transpose(speed)
                stacked[h, at, :] = term if e == 0 else stacked[h, at, :] + term

    by_segment = weight_columns(table)
    build(arrived, by_segment, tile, 0, onehot, cells)
    start(*total(cells, onehot, 0, 0), 0, 0, keeps, adds, change)
    build(arrived, by_segment, tile, 1, onehot, cells)
    start(*total(cells, onehot, 0, 256), 0, 256, keeps, adds, change)
    sweep(0)
    start(*total(cells, onehot, 1, 0), 1, 0, keeps, adds, change)
    sweep(0)
    start(*total(cells, onehot, 1, 256), 1, 256, keeps, adds, change)
    sweep(0)
    for copy in copies:
        copy.wait()
    stack(0)
    for k in range(SWEEPS - 1):
        sweep(1)
    stack(1)

    def deal(out, core_of):
        first = pl.multiple_of(core_of * SHARE, SHARE)
        for g in range(YS * ZS):
            at = pl.ds(first + g * (CS * SHARE), SHARE)
            k = g ^ (Y_FIRST * ZS + Z_FIRST)
            for h in range(2):
                part = slice(h * LANES, (h + 1) * LANES)
                out[k, 0, :, part] = stacked[h, at, :]
                out[k, 1, :, part] = valid[0, h, at, :] + valid[1, h, at, :]

    deal(send, 1 - core)
    deal(keep, core)


def maps_of(arrived, table, source_row, source_col, valid):
    f32 = jnp.float32
    shares = jax.ShapeDtypeStruct((YS * ZS, 2, SHARE, COLS), f32)
    vmem, smem = pl.BlockSpec(memory_space=pltpu.VMEM), pl.BlockSpec(memory_space=pltpu.SMEM)
    wide = pltpu.VMEM((EVENTS, LINES, SPAN, LANES), f32)
    padded = pltpu.VMEM((EVENTS, LINES, SPAN + 2 * PAD, LANES), f32)
    return pl.pallas_call(
        work,
        out_shape=(shares, shares),
        in_specs=[vmem, vmem, smem, smem, pl.BlockSpec(memory_space=pltpu.HBM)],
        out_specs=(vmem, vmem),
        scratch_shapes=[
            pltpu.VMEM((EVENTS, ROWS, LISTS * SLOTS), jnp.bfloat16),
            pltpu.VMEM((EVENTS, 3 * SPAN, LISTS * SLOTS), jnp.bfloat16),
            wide, wide, padded, padded,
            pltpu.VMEM((EVENTS, 2, ROWS, LANES), f32),
            pltpu.VMEM((2, ROWS, LANES), f32),
            pltpu.SemaphoreType.DMA((2 * EVENTS,)),
        ],
        compiler_params=pltpu.CompilerParams(vmem_limit_bytes=53760 * 1024),
        name="maps",
    )(arrived, table, source_row, source_col, valid)


def packed(times, kernels, blocks, dests, counts):
    vmem, smem = pl.BlockSpec(memory_space=pltpu.VMEM), pl.BlockSpec(memory_space=pltpu.SMEM)
    return pl.pallas_call(
        pack,
        out_shape=jax.ShapeDtypeStruct((LISTS, 16, LANES), jnp.float32),
        in_specs=[vmem, vmem, vmem, vmem, smem],
        out_specs=vmem,
        name="pack",
    )(times, kernels, blocks, dests, counts)


def on_device(times, kernels, blocks, dests, counts, table, source_row, source_col, valid):
    outgoing = packed(times, kernels, blocks, dests.reshape(EVENTS, 1, SLOTS), counts)
    arrived = lax.all_to_all(outgoing, TILE, 0, 0, tiled=True, axis_index_groups=order(TILE_FIRST, LISTS))
    send, keep = maps_of(arrived, table, source_row, source_col, valid)
    both = keep + lax.ppermute(send, "c", [(0, 1), (1, 0)])
    both = both.reshape(YS, ZS, 2, SHARE, COLS)
    both = jnp.sum(lax.all_to_all(both, "y", 0, 0, tiled=True, axis_index_groups=order(Y_FIRST, YS)), axis=0)
    both = jnp.sum(lax.all_to_all(both, "z", 0, 0, tiled=True, axis_index_groups=order(Z_FIRST, ZS)), axis=0)
    return both[0] / (1.0 + both[1])


def solution(mesh):
    split = Mesh(np.asarray(mesh.devices).reshape(YS, ZS, CS, XS * WS), EV + (TILE,))
    placed = (
        P(TILE, EV, None),
        P(TILE, EV, None),
        P(TILE, EV, None),
        P(TILE, EV, None, None),
        P(TILE, EV),
        P(),
        P(EV),
        P(EV),
        P(EV, None, TILE),
    )
    return jax.shard_map(on_device, mesh=split, in_specs=placed, out_specs=P(EV, TILE), check_vma=False)
```
